128 devices in a mesh: inp: 4 (over y), tm: 32 (over x, z, core).
Axes of the slice: x: 4, y: 4, z: 4, core: 2. Of those that a mesh axis runs over, the one named last changes fastest.
Arguments:
- voltages: bfloat16 [1024, 128, 2048], P('inp', 'tm'), may hold values from -6 to 6
- window: float32 [4, 2048], replicated, may hold values from -0.0625 to 0.0625
Outputs:
- visibilities: float32 [512, 1024, 1024], P('tm', 'inp')
The draws below stay inside these ranges and needn't reach their ends.
All inputs are finite; a program needn't handle non-finite values.
Results may differ from the reference program's by a relative error of at most 0.0051.
Values may be sent and summed in bfloat16 or wider, within the bound.
No kernel may reach another device: no remote copies, remote signals or barrier semaphores. Data moves between devices by JAX's collectives and lax.ppermute only.
A program may use at most 128 MiB of HBM per device.

```python
import math
import jax
import jax.numpy as jnp
from jax import lax

FRAME = 2048
TAPS = 4
INPUTS = 1024
CH_FIRST = 512
CHAN = 512
TIMES = 128


def steps_of(own_key, extent, shards, least, largest):
    loudness = 1.0
    for position, parts in shards:
        steps = jax.random.uniform(jax.random.fold_in(jax.random.fold_in(own_key, 6), position), (parts,), jnp.float32, least / len(shards), largest / len(shards))
        loudness = loudness * jnp.repeat(jnp.exp(steps), extent[position] // parts).reshape((-1,) + (1,) * (len(extent) - 1 - position))
    return loudness


def gaussian(rng, shape, scale, bound, cuts=(), kind=jnp.bfloat16):
    entries = scale * jax.random.normal(rng, shape, jnp.float32)
    if cuts:
        entries = entries * steps_of(rng, shape, cuts, -0.22, 0.18)
    return jnp.clip(entries, -bound, bound).astype(kind)


def setup_inputs(seed: int = 0) -> dict:
    key_list = jax.random.split(jax.random.key(seed), 3)
    voltages = gaussian(key_list[0], (INPUTS, TIMES, FRAME), 1.0, 6.0, ((0, 4), (1, 32)))
    window = gaussian(key_list[1], (TAPS, FRAME), (TAPS * FRAME) ** -0.5, 0.0625, (), jnp.float32)
    return dict(voltages=voltages, window=window)


def tables(window):
    index = jnp.arange(FRAME, dtype=jnp.int32)
    bins = CH_FIRST + jnp.arange(CHAN, dtype=jnp.int32)
    phase = (index[:, None] * bins[None, :]) % FRAME
    angle = (2.0 * math.pi / FRAME) * phase.astype(jnp.float32)
    table = jnp.concatenate([jnp.cos(angle), -jnp.sin(angle)], axis=1)
    return (window[:, :, None] * table[None, :, :]).astype(jnp.bfloat16)


def reference(voltages, window):
    filt = tables(window)
    spectra = jnp.zeros((INPUTS, TIMES, 2 * CHAN), jnp.float32)
    for tap in range(TAPS):
        frames = voltages[:, :TIMES - tap, :].reshape(-1, FRAME).astype(jnp.float32)
        term = jnp.dot(frames, filt[tap].astype(jnp.float32), precision=lax.Precision.HIGHEST)
        spectra = spectra.at[:, tap:, :].add(term.reshape(INPUTS, TIMES - tap, 2 * CHAN))
    rounded = spectra.astype(jnp.bfloat16)
    real_part = rounded[:, :, :CHAN]
    imag_part = rounded[:, :, CHAN:]
    row_ids = jnp.arange(INPUTS, dtype=jnp.int32)
    upper = row_ids[:, None] <= row_ids[None, :]

    def one_channel(chan):
        xr = lax.dynamic_index_in_dim(real_part, chan, 2, keepdims=False).astype(jnp.float32)
        xi = lax.dynamic_index_in_dim(imag_part, chan, 2, keepdims=False).astype(jnp.float32)
        left = jnp.concatenate([xr, xi], axis=1)
        turned = jnp.concatenate([xi, -xr], axis=1)
        re_plane = jnp.dot(left, left.T, precision=lax.Precision.HIGHEST)
        im_plane = jnp.dot(turned, left.T, precision=lax.Precision.HIGHEST)
        return jnp.where(upper, re_plane, im_plane) * (1.0 / TIMES)

    return lax.map(one_channel, jnp.arange(CHAN, dtype=jnp.int32))
```

```python
import numpy as np

import jax
import jax.numpy as jnp
from jax import lax
from jax.experimental import pallas as pl
from jax.experimental.pallas import tpu as pltpu
from jax.sharding import PartitionSpec as P

FRAME = 2048
TAPS = 4
CH_FIRST = 512
QUARTER = FRAME // 4
CLASSES = 4
F32 = jnp.float32
BF16 = jnp.bfloat16
ROWS = 256
LANES = 256
VMEM = 48 * 1024 * 1024


def halves(x):
    high = x.astype(BF16)
    return high, (x - high.astype(F32)).astype(BF16)


def dft_tables():
    tables = []
    index = np.arange(QUARTER)
    for b in range(CLASSES):
        bins = CH_FIRST + b + CLASSES * np.arange(128)
        phase = (bins[:, None] * index[None, :]) % FRAME
        turn = np.exp(-2j * np.pi / FRAME * phase)
        if b % 2:
            turn = np.concatenate([turn, turn * (-1j if b == 1 else 1j)], axis=1)
        tables.append(np.stack([turn.real, turn.imag], axis=1).reshape(2 * len(bins), -1))
    both = np.concatenate(tables, axis=1)
    high = both.astype(BF16)
    return high, (both - high.astype(np.float64)).astype(BF16)


def spectra_kernel(times, groups, fine, v_hbm, w_ref, *refs):
    n = 2 if fine else 1
    tables_hbm, refs = refs[:n], refs[n:]
    outs, refs = refs[: len(groups)], refs[len(groups) :]
    frames, high, low, v_ref = refs[:4]
    tables = refs[4 : 4 + n]
    v_sem, table_sem = refs[4 + n :]
    classes = [b for group in groups for b in group]
    block = ROWS // TAPS
    sub = 16
    v_copies = [
        pltpu.make_async_copy(v_hbm.at[pl.ds(i * block, block)], v_ref.at[pl.ds(i * block, block)], v_sem.at[i])
        for i in range(ROWS // block)
    ]
    table_copies = [pltpu.make_async_copy(tables_hbm[k], tables[k], table_sem.at[k]) for k in range(n)]
    for copy in v_copies + table_copies:
        copy.start()

    to = lax.broadcasted_iota(jnp.int32, (ROWS, ROWS), 0)
    at = lax.broadcasted_iota(jnp.int32, (ROWS, ROWS), 1)
    sort = jnp.where(at == (to % block) * TAPS + to // block, 1.0, 0.0).astype(BF16)

    def per_block(i):
        v_copies[i].wait()
        x = v_ref[pl.ds(i * block, block)].reshape(ROWS, FRAME)
        frames[...] = jnp.dot(sort, x, preferred_element_type=F32)

        def per_rows(r, carry):
            for col in range(QUARTER // 128):
                spans = [pl.ds(m * QUARTER + col * 128, 128) for m in range(4)]
                taps = [[w_ref[pl.ds(j, 1), span] for span in spans] for j in range(TAPS)]
                parts = [
                    [frames[pl.ds(s * block + r * sub, sub), span] for span in spans]
                    for s in range(TAPS)
                ]
                for slot, t in enumerate(times):
                    u = []
                    for m in range(4):
                        terms = [taps[j][m] * parts[t - j][m] for j in range(TAPS) if 0 <= t - j < TAPS]
                        total = terms[0]
                        for term in terms[1:]:
                            total = total + term
                        u.append(total)
                    even, odd = u[0] + u[2], u[1] + u[3]
                    folded = {}
                    if 0 in classes:
                        folded[0] = even + odd
                    if 2 in classes:
                        folded[1] = even - odd
                    if 1 in classes or 3 in classes:
                        folded[2] = u[0] - u[2]
                        folded[3] = u[1] - u[3]
                    for f, value in folded.items():
                        where = slot, pl.ds(i * block + r * sub, sub), pl.ds(f * QUARTER + col * 128, 128)
                        if fine:
                            high[where], low[where] = halves(value)
                        else:
                            high[where] = value.astype(BF16)
            return carry

        lax.fori_loop(0, block // sub, per_rows, 0)

    for i in range(ROWS // block):
        per_block(i)
    spans = [slice(0, 512), slice(1024, 2048), slice(512, 1024), slice(1024, 2048)]
    columns = [slice(0, 512), slice(512, 1536), slice(1536, 2048), slice(2048, 3072)]
    contract = (((1,), (1,)), ((), ()))
    for copy in table_copies:
        copy.wait()

    def per_time(slot, carry):
        for b in classes:
            h = high[slot, :, spans[b]]
            table = tables[0][:, columns[b]]
            total = lax.dot_general(table, h, contract, preferred_element_type=F32)
            if fine:
                l = low[slot, :, spans[b]]
                total += lax.dot_general(table, l, contract, preferred_element_type=F32)
                total += lax.dot_general(tables[1][:, columns[b]], h, contract, preferred_element_type=F32)
            for group, out in zip(groups, outs):
                if b in group:
                    out[group.index(b) * len(times) + slot] = total.astype(out.dtype)
        return carry

    lax.fori_loop(0, len(times), per_time, 0)


def spectra(v, window, tables, times, groups, fine):
    def kernel(*refs):
        spectra_kernel(times, groups, fine, *refs)

    n = len(times)
    tables = tables if fine else tables[:1]
    anywhere = pl.BlockSpec(memory_space=pltpu.HBM)
    return pl.pallas_call(
        kernel,
        out_shape=[jax.ShapeDtypeStruct((n * len(g), 256, LANES), F32 if fine else BF16) for g in groups],
        in_specs=[anywhere, pl.BlockSpec()] + [anywhere] * len(tables),
        scratch_shapes=[
            pltpu.VMEM((ROWS, FRAME), F32),
            pltpu.VMEM((n, ROWS, FRAME), BF16),
            pltpu.VMEM((n if fine else 1, ROWS, FRAME), BF16),
            pltpu.VMEM((ROWS, TAPS, FRAME), BF16),
            *[pltpu.VMEM(t.shape, BF16) for t in tables],
            pltpu.SemaphoreType.DMA((4,)),
            pltpu.SemaphoreType.DMA((len(tables),)),
        ],
        compiler_params=pltpu.CompilerParams(vmem_limit_bytes=VMEM),
        cost_estimate=pl.CostEstimate(flops=n * sum(map(len, groups)) * 300000000, bytes_accessed=12 << 20, transcendentals=0),
        name="spectra",
    )(v, window, *tables)


def combine_kernel(order, parts, *refs):
    own, halo = refs[: len(order)], refs[len(order)]
    rows = refs[-1]
    outs = refs[len(refs) - 1 - parts : -1]
    size = 32 // parts
    for k, halo_at in enumerate(order):
        for half in range(LANES // 128):
            span = pl.ds(half * 128, 128)
            for t in range(TAPS):
                value = own[k][t, :, span]
                if t < TAPS - 1:
                    value = value + halo[halo_at * (TAPS - 1) + t, :, span].astype(F32)
                rows[half, pl.ds(t, 256, stride=TAPS), :] = value
            for part in range(parts):
                value = rows[half, pl.ds(part * size * 32, size * 32)].astype(BF16)
                outs[part][:, pl.ds(k * 32, 32), span] = value.reshape(size, 32, 128)


def combine(own, halo, order, parts, after=()):
    n = len(order)

    def kernel(*refs):
        combine_kernel(order, parts, *refs)

    return pl.pallas_call(
        kernel,
        out_shape=[jax.ShapeDtypeStruct((32 // parts, 32 * n, LANES), BF16)] * parts,
        in_specs=[pl.BlockSpec()] * (n + 1) + [pl.BlockSpec(memory_space=pltpu.HBM)] * len(after),
        scratch_shapes=[pltpu.VMEM((LANES // 128, 1024, 128), F32)],
        compiler_params=pltpu.CompilerParams(vmem_limit_bytes=VMEM),
        cost_estimate=pl.CostEstimate(flops=n << 20, bytes_accessed=n * (2 << 20), transcendentals=0),
        name="combine",
    )(*own, halo, *after)


def take(parts, after=()):
    def kernel(*refs):
        for k in range(len(parts)):
            refs[len(refs) - len(parts) + k][...] = refs[k][...]

    in_specs = [pl.BlockSpec(shape, lambda g, at=at: at) for _, shape, at in parts]
    out_specs = [pl.BlockSpec(shape, lambda g: (0, 0, 0)) for _, shape, _ in parts]
    return pl.pallas_call(
        kernel,
        out_shape=[jax.ShapeDtypeStruct(shape, BF16) for _, shape, _ in parts],
        grid=(1,),
        in_specs=in_specs + [pl.BlockSpec(memory_space=pltpu.HBM)] * len(after),
        out_specs=out_specs,
        compiler_params=pltpu.CompilerParams(vmem_limit_bytes=VMEM),
        cost_estimate=pl.CostEstimate(flops=0, bytes_accessed=2 << 20, transcendentals=0),
        name="take",
    )(*[array for array, _, _ in parts], *after)


def pack_kernel(own, right, far_a, far_b, left, *refs):
    out = refs[-1]
    out[:, 0:32] = own[...]
    out[:, 32:64] = right[...]
    out[:, 96:128] = left[...]

    @pl.when(pl.program_id(0) < 2)
    def _():
        out[:, 64:96] = far_a[...]

    @pl.when(pl.program_id(0) >= 2)
    def _():
        out[:, 64:96] = far_b[...]


def pack(own, planes, after=()):
    part = (8, 32, LANES)
    whole = pl.BlockSpec(part, lambda g: (g, 0, 0))
    return pl.pallas_call(
        pack_kernel,
        out_shape=jax.ShapeDtypeStruct((32, 128, LANES), BF16),
        grid=(4,),
        in_specs=[
            whole,
            whole,
            pl.BlockSpec(part, lambda g: (jnp.minimum(g, 1), 0, 0)),
            pl.BlockSpec(part, lambda g: (jnp.maximum(g - 2, 0), 0, 0)),
            whole,
        ]
        + [pl.BlockSpec(memory_space=pltpu.HBM)] * len(after),
        out_specs=pl.BlockSpec((8, 128, LANES), lambda g: (g, 0, 0)),
        compiler_params=pltpu.CompilerParams(vmem_limit_bytes=VMEM),
        cost_estimate=pl.CostEstimate(flops=0, bytes_accessed=4 << 20, transcendentals=0),
        name="pack",
    )(own, *planes[1], *planes[2], *planes[3], *after)


def correlate_kernel(steps, n_own, whole, place, *refs):
    out = refs[-1]
    y = place[0]
    scale = 1.0 / 128
    ids = lax.broadcasted_iota(jnp.int32, (8, 1), 0)
    sign = jnp.where(ids < 4, 1.0, -1.0)
    row = lax.broadcasted_iota(jnp.int32, (ROWS, ROWS), 0)
    col = lax.broadcasted_iota(jnp.int32, (ROWS, ROWS), 1)

    def pair(ref):
        return ref[...].astype(F32).reshape(ref.shape[0], 2, 8, LANES)

    def flat(x):
        return x.reshape(x.shape[0] * 8, LANES)

    def times_of(plane, other):
        return jnp.dot(plane, other, preferred_element_type=F32) * scale

    mine = [pair(ref) for ref in refs[:n_own]]
    planes = []
    for i in range(2):
        p = jnp.concatenate([x[:, i] for x in mine], axis=0)
        flipped = pltpu.roll(p, 4, 1) * sign
        if whole:
            planes.append((flat(p).astype(BF16).T, flat(flipped).astype(BF16).T))
        else:
            planes.append((p, flipped))

    def products(step, pieces):
        pieces = [pair(refs[k]) for k in pieces]
        q = lax.rem(y + step, 4)
        for i in range(2):
            real, imag = planes[i]
            if step == 0:
                same = jnp.concatenate([flat(x[:, i]) for x in mine], axis=0).astype(BF16)
                yield i, y, jnp.where(row <= col, times_of(real, same), times_of(imag, same))
            else:
                plane = jnp.where(q < y, imag, real)
                if not whole:
                    plane = flat(plane).astype(BF16).T
                other = jnp.concatenate([flat(x[:, i]) for x in pieces], axis=0).astype(BF16)
                yield i, q, times_of(plane, other)

    if whole:
        for step, pieces in steps:
            for i, q, value in products(step, pieces):
                out[i, 0, :, pl.ds(pl.multiple_of(q * 256, 256), 256)] = value
    else:
        for e, (step, pieces) in enumerate(steps):

            @pl.when(pl.program_id(1) == e)
            def _():
                for i, _, value in products(step, pieces):
                    out[i, 0] = value


def correlate(place, b, own, others, before, whole, base=0, after=()):
    def spec(array, step):
        row = {32: 0, 64: base, 128: step}[array.shape[1]]
        return pl.BlockSpec((array.shape[0], 16, LANES), lambda g, *rest: (0, 2 * row + g, 0))

    if not isinstance(own, (list, tuple)):
        own = [own]
    in_specs = [spec(array, 0) for array in own]
    args = [place, *own]
    steps = []
    for step, arrays in others.items():
        steps.append((step, tuple(range(len(args) - 1, len(args) - 1 + len(arrays)))))
        for array in arrays:
            in_specs.append(spec(array, step))
            args.append(array)
    aliases = {}
    if before is not None:
        in_specs.append(pl.BlockSpec(memory_space=pltpu.HBM))
        aliases = {len(args): 0}
        args.append(before)

    in_specs += [pl.BlockSpec(memory_space=pltpu.HBM)] * len(after)
    args += after

    def kernel(*refs):
        correlate_kernel(steps, len(own), whole, *refs)

    first = steps[0][0]
    if whole:
        grid = (2,)
        out_spec = pl.BlockSpec((2, 1, ROWS, 1024), lambda g, y: (g, b, 0, 0))
    else:
        grid = (2, len(steps))
        out_spec = pl.BlockSpec((2, 1, ROWS, 256), lambda g, e, y: (g, b, 0, lax.rem(y[0] + first + e, 4)))
    return pl.pallas_call(
        kernel,
        out_shape=jax.ShapeDtypeStruct((4, 4, ROWS, 1024), F32),
        grid_spec=pltpu.PrefetchScalarGridSpec(
            num_scalar_prefetch=1, grid=grid, in_specs=in_specs, out_specs=out_spec
        ),
        input_output_aliases=aliases,
        compiler_params=pltpu.CompilerParams(vmem_limit_bytes=60 * 1024 * 1024),
        cost_estimate=pl.CostEstimate(flops=len(steps) * 160000000, bytes_accessed=6 << 20, transcendentals=0),
        name="correlate",
    )(*args)


def body(v, window):
    groups = lax.axis_size("tm")
    ring = lax.axis_size("inp")
    tables = [jnp.asarray(t) for t in dft_tables()]
    place = lax.axis_index("inp").astype(jnp.int32).reshape(1)
    later = [(i, i + 1) for i in range(groups - 1)]

    def up(x):
        return lax.ppermute(x, "inp", [(i, (i + 1) % ring) for i in range(ring)])

    def down(x):
        return lax.ppermute(x, "inp", [(i, (i - 1) % ring) for i in range(ring)])

    def swap(x):
        return lax.all_to_all(x, "tm", split_axis=0, concat_axis=0, tiled=True)

    (passed,) = spectra(v, window, tables, (4, 5, 6), ((1, 3, 2, 0),), False)
    halo = lax.ppermute(passed, "tm", later)
    own = spectra(v, window, tables, (0, 1, 2, 3), ((1,), (3,), (2,), (0,)), True)
    lower, upper, half = (0, 0, 0), (1, 0, 0), (16, 32, LANES)

    (early,) = combine(own[3:], halo, (3,), 1)
    (rows,) = combine(own[:3], halo, (0, 1, 2), 1, (early,))
    late = swap(rows)
    left, right = up(early), down(early)
    first, second = take([(left, half, lower), (right, half, upper)])
    early = pack(early, {1: [right], 2: [up(first), down(second)], 3: [left]})
    odd, even = take([(late, (32, 64, LANES), (0, 0, 0)), (late, (32, 32, LANES), (0, 2, 0))])
    odd_left, odd_right = up(odd), down(odd)
    even_left, even_right = up(even), down(even)
    early = swap(early)

    whole = (32, 32, LANES)
    near = {0: [], 1: [odd_right], 3: [odd_left]}
    out = correlate(place, 0, early, {0: [], 1: [early], 2: [early], 3: [early]}, None, True, 0, [odd_left, odd_right])
    first, second = take([(odd_left, whole, (0, 0, 0)), (odd_right, whole, (0, 1, 0))], (out,))
    odd_far = up(first), down(second)
    out = correlate(place, 1, odd, near, out, True, 0)
    out = correlate(place, 3, odd, near, out, True, 1)
    first, second = take([(even_left, half, lower), (even_right, half, upper)], (out,))
    even_far = [up(first), down(second)]
    out = correlate(place, 2, even, {0: [], 1: [even_right], 3: [even_left]}, out, True, 0, list(odd_far))
    out = correlate(place, 1, odd, {2: [odd_far[0]]}, out, False, 0)
    out = correlate(place, 3, odd, {2: [odd_far[1]]}, out, False, 1)
    out = correlate(place, 2, even, {2: even_far}, out, False, 0)
    return out.reshape(16, ROWS, 1024)


def solution(mesh):
    in_specs = (P("inp", "tm", None), P())
    out_specs = P("tm", "inp", None)
    return jax.shard_map(body, mesh=mesh, in_specs=in_specs, out_specs=out_specs, check_vma=False)
```

```python
import numpy as np

import jax
import jax.numpy as jnp
from jax import lax
from jax.experimental import pallas as pl
from jax.experimental.pallas import tpu as pltpu
from jax.sharding import PartitionSpec as P

FRAME = 2048
TAPS = 4
CH_FIRST = 512
QUARTER = FRAME // 4
CLASSES = 4
F32 = jnp.float32
BF16 = jnp.bfloat16
ROWS = 256
LANES = 256
VMEM = 48 * 1024 * 1024


def halves(x):
    high = x.astype(BF16)
    return high, (x - high.astype(F32)).astype(BF16)


def dft_tables():
    tables = []
    index = np.arange(QUARTER)
    for b in range(CLASSES):
        bins = CH_FIRST + b + CLASSES * np.arange(128)
        phase = (bins[:, None] * index[None, :]) % FRAME
        turn = np.exp(-2j * np.pi / FRAME * phase)
        if b % 2:
            turn = np.concatenate([turn, turn * (-1j if b == 1 else 1j)], axis=1)
        tables.append(np.stack([turn.real, turn.imag], axis=1).reshape(2 * len(bins), -1))
    both = np.concatenate(tables, axis=1)
    high = both.astype(BF16)
    return high, (both - high.astype(np.float64)).astype(BF16)


def spectra_kernel(times, groups, fine, inputs, v_hbm, w_ref, *refs):
    n = 2 if fine else 1
    tables_hbm, refs = refs[:n], refs[n:]
    outs, refs = refs[: len(groups)], refs[len(groups) :]
    frames, high, low, v_ref = refs[:4]
    tables = refs[4 : 4 + n]
    v_sem, table_sem = refs[4 + n :]
    classes = [b for group in groups for b in group]
    block = ROWS // TAPS
    sub = 16
    v_copies = [
        pltpu.make_async_copy(
            v_hbm.at[pl.ds(inputs.start + i * block, block)], v_ref.at[pl.ds(i * block, block)], v_sem.at[i]
        )
        for i in range(len(inputs) // block)
    ]
    table_copies = [pltpu.make_async_copy(tables_hbm[k], tables[k], table_sem.at[k]) for k in range(n)]
    for copy in v_copies + table_copies:
        copy.start()

    to = lax.broadcasted_iota(jnp.int32, (ROWS, ROWS), 0)
    at = lax.broadcasted_iota(jnp.int32, (ROWS, ROWS), 1)
    sort = jnp.where(at == (to % block) * TAPS + to // block, 1.0, 0.0).astype(BF16)

    def per_block(i):
        v_copies[i].wait()
        x = v_ref[pl.ds(i * block, block)].reshape(ROWS, FRAME)
        frames[...] = jnp.dot(sort, x, preferred_element_type=F32)

        def per_rows(r, carry):
            for col in range(QUARTER // 128):
                spans = [pl.ds(m * QUARTER + col * 128, 128) for m in range(4)]
                taps = [[w_ref[pl.ds(j, 1), span] for span in spans] for j in range(TAPS)]
                parts = [
                    [frames[pl.ds(s * block + r * sub, sub), span] for span in spans]
                    for s in range(TAPS)
                ]
                for slot, t in enumerate(times):
                    u = []
                    for m in range(4):
                        terms = [taps[j][m] * parts[t - j][m] for j in range(TAPS) if 0 <= t - j < TAPS]
                        total = terms[0]
                        for term in terms[1:]:
                            total = total + term
                        u.append(total)
                    even, odd = u[0] + u[2], u[1] + u[3]
                    folded = {}
                    if 0 in classes:
                        folded[0] = even + odd
                    if 2 in classes:
                        folded[1] = even - odd
                    if 1 in classes or 3 in classes:
                        folded[2] = u[0] - u[2]
                        folded[3] = u[1] - u[3]
                    for f, value in folded.items():
                        where = slot, pl.ds(i * block + r * sub, sub), pl.ds(f * QUARTER + col * 128, 128)
                        if fine:
                            high[where], low[where] = halves(value)
                        else:
                            high[where] = value.astype(BF16)
            return carry

        lax.fori_loop(0, block // sub, per_rows, 0)

    for i in range(len(inputs) // block):
        per_block(i)
    spans = [slice(0, 512), slice(1024, 2048), slice(512, 1024), slice(1024, 2048)]
    columns = [slice(0, 512), slice(512, 1536), slice(1536, 2048), slice(2048, 3072)]
    contract = (((1,), (1,)), ((), ()))
    for copy in table_copies:
        copy.wait()

    def per_time(slot, carry):
        for b in classes:
            h = high[slot, :, spans[b]]
            table = tables[0][:, columns[b]]
            total = lax.dot_general(table, h, contract, preferred_element_type=F32)
            if fine:
                l = low[slot, :, spans[b]]
                total += lax.dot_general(table, l, contract, preferred_element_type=F32)
                total += lax.dot_general(tables[1][:, columns[b]], h, contract, preferred_element_type=F32)
            for group, out in zip(groups, outs):
                if b in group:
                    out[group.index(b) * len(times) + slot] = total.astype(out.dtype)
        return carry

    lax.fori_loop(0, len(times), per_time, 0)


def spectra(v, window, tables, times, groups, fine, inputs=range(ROWS)):
    def kernel(*refs):
        spectra_kernel(times, groups, fine, inputs, *refs)

    n, size = len(times), len(inputs)
    tables = tables if fine else tables[:1]
    anywhere = pl.BlockSpec(memory_space=pltpu.HBM)
    return pl.pallas_call(
        kernel,
        out_shape=[jax.ShapeDtypeStruct((n * len(g), 256, size), F32 if fine else BF16) for g in groups],
        in_specs=[anywhere, pl.BlockSpec()] + [anywhere] * len(tables),
        scratch_shapes=[
            pltpu.VMEM((ROWS, FRAME), F32),
            pltpu.VMEM((n, size, FRAME), BF16),
            pltpu.VMEM((n if fine else 1, size, FRAME), BF16),
            pltpu.VMEM((size, TAPS, FRAME), BF16),
            *[pltpu.VMEM(t.shape, BF16) for t in tables],
            pltpu.SemaphoreType.DMA((size // (ROWS // TAPS),)),
            pltpu.SemaphoreType.DMA((len(tables),)),
        ],
        compiler_params=pltpu.CompilerParams(vmem_limit_bytes=VMEM),
        cost_estimate=pl.CostEstimate(flops=n * sum(map(len, groups)) * 300000000, bytes_accessed=12 << 20, transcendentals=0),
        name="spectra",
    )(v, window, *tables)


def combine_kernel(order, parts, *refs):
    own, halo = refs[: len(order)], refs[len(order) : len(order) + 2]
    rows = refs[-1]
    outs = refs[len(refs) - 1 - parts : -1]
    size = 32 // parts
    for k, halo_at in enumerate(order):
        for half in range(LANES // 128):
            span = pl.ds(half * 128, 128)
            for t in range(TAPS):
                value = own[k][t, :, span]
                if t < TAPS - 1:
                    value = value + halo[half][halo_at * (TAPS - 1) + t].astype(F32)
                rows[half, pl.ds(t, 256, stride=TAPS), :] = value
            for part in range(parts):
                value = rows[half, pl.ds(part * size * 32, size * 32)].astype(BF16)
                outs[part][:, pl.ds(k * 32, 32), span] = value.reshape(size, 32, 128)


def combine(own, halo, order, parts, after=()):
    n = len(order)

    def kernel(*refs):
        combine_kernel(order, parts, *refs)

    return pl.pallas_call(
        kernel,
        out_shape=[jax.ShapeDtypeStruct((32 // parts, 32 * n, LANES), BF16)] * parts,
        in_specs=[pl.BlockSpec()] * (n + 2) + [pl.BlockSpec(memory_space=pltpu.HBM)] * len(after),
        scratch_shapes=[pltpu.VMEM((LANES // 128, 1024, 128), F32)],
        compiler_params=pltpu.CompilerParams(vmem_limit_bytes=VMEM),
        cost_estimate=pl.CostEstimate(flops=n << 20, bytes_accessed=n * (2 << 20), transcendentals=0),
        name="combine",
    )(*own, *halo, *after)


def take(parts, after=()):
    def kernel(*refs):
        for k in range(len(parts)):
            refs[len(refs) - len(parts) + k][...] = refs[k][...]

    in_specs = [pl.BlockSpec(shape, lambda g, at=at: at) for _, shape, at in parts]
    out_specs = [pl.BlockSpec(shape, lambda g: (0, 0, 0)) for _, shape, _ in parts]
    return pl.pallas_call(
        kernel,
        out_shape=[jax.ShapeDtypeStruct(shape, BF16) for _, shape, _ in parts],
        grid=(1,),
        in_specs=in_specs + [pl.BlockSpec(memory_space=pltpu.HBM)] * len(after),
        out_specs=out_specs,
        compiler_params=pltpu.CompilerParams(vmem_limit_bytes=VMEM),
        cost_estimate=pl.CostEstimate(flops=0, bytes_accessed=2 << 20, transcendentals=0),
        name="take",
    )(*[array for array, _, _ in parts], *after)


def pack_kernel(own, right, far_a, far_b, left, *refs):
    out = refs[-1]
    out[:, 0:32] = own[...]
    out[:, 32:64] = right[...]
    out[:, 96:128] = left[...]

    @pl.when(pl.program_id(0) < 2)
    def _():
        out[:, 64:96] = far_a[...]

    @pl.when(pl.program_id(0) >= 2)
    def _():
        out[:, 64:96] = far_b[...]


def pack(own, planes, after=()):
    part = (8, 32, LANES)
    whole = pl.BlockSpec(part, lambda g: (g, 0, 0))
    return pl.pallas_call(
        pack_kernel,
        out_shape=jax.ShapeDtypeStruct((32, 128, LANES), BF16),
        grid=(4,),
        in_specs=[
            whole,
            whole,
            pl.BlockSpec(part, lambda g: (jnp.minimum(g, 1), 0, 0)),
            pl.BlockSpec(part, lambda g: (jnp.maximum(g - 2, 0), 0, 0)),
            whole,
        ]
        + [pl.BlockSpec(memory_space=pltpu.HBM)] * len(after),
        out_specs=pl.BlockSpec((8, 128, LANES), lambda g: (g, 0, 0)),
        compiler_params=pltpu.CompilerParams(vmem_limit_bytes=VMEM),
        cost_estimate=pl.CostEstimate(flops=0, bytes_accessed=4 << 20, transcendentals=0),
        name="pack",
    )(own, *planes[1], *planes[2], *planes[3], *after)


def correlate_kernel(steps, n_own, whole, place, *refs):
    out = refs[-1]
    y = place[0]
    scale = 1.0 / 128
    ids = lax.broadcasted_iota(jnp.int32, (8, 1), 0)
    sign = jnp.where(ids < 4, 1.0, -1.0)
    row = lax.broadcasted_iota(jnp.int32, (ROWS, ROWS), 0)
    col = lax.broadcasted_iota(jnp.int32, (ROWS, ROWS), 1)

    def pair(ref):
        return ref[...].astype(F32).reshape(ref.shape[0], 2, 8, LANES)

    def flat(x):
        return x.reshape(x.shape[0] * 8, LANES)

    def times_of(plane, other):
        return jnp.dot(plane, other, preferred_element_type=F32) * scale

    mine = [pair(ref) for ref in refs[:n_own]]
    planes = []
    for i in range(2):
        p = jnp.concatenate([x[:, i] for x in mine], axis=0)
        flipped = pltpu.roll(p, 4, 1) * sign
        if whole:
            planes.append((flat(p).astype(BF16).T, flat(flipped).astype(BF16).T))
        else:
            planes.append((p, flipped))

    def products(step, pieces):
        pieces = [pair(refs[k]) for k in pieces]
        q = lax.rem(y + step, 4)
        for i in range(2):
            real, imag = planes[i]
            if step == 0:
                same = jnp.concatenate([flat(x[:, i]) for x in mine], axis=0).astype(BF16)
                yield i, y, jnp.where(row <= col, times_of(real, same), times_of(imag, same))
            else:
                plane = jnp.where(q < y, imag, real)
                if not whole:
                    plane = flat(plane).astype(BF16).T
                other = jnp.concatenate([flat(x[:, i]) for x in pieces], axis=0).astype(BF16)
                yield i, q, times_of(plane, other)

    if whole:
        for step, pieces in steps:
            for i, q, value in products(step, pieces):
                out[i, 0, :, pl.ds(pl.multiple_of(q * 256, 256), 256)] = value
    else:
        for e, (step, pieces) in enumerate(steps):

            @pl.when(pl.program_id(1) == e)
            def _():
                for i, _, value in products(step, pieces):
                    out[i, 0] = value


def correlate(place, b, own, others, before, whole, base=0, after=()):
    def spec(array, step):
        row = {32: 0, 64: base, 128: step}[array.shape[1]]
        return pl.BlockSpec((array.shape[0], 16, LANES), lambda g, *rest: (0, 2 * row + g, 0))

    if not isinstance(own, (list, tuple)):
        own = [own]
    in_specs = [spec(array, 0) for array in own]
    args = [place, *own]
    steps = []
    for step, arrays in others.items():
        steps.append((step, tuple(range(len(args) - 1, len(args) - 1 + len(arrays)))))
        for array in arrays:
            in_specs.append(spec(array, step))
            args.append(array)
    aliases = {}
    if before is not None:
        in_specs.append(pl.BlockSpec(memory_space=pltpu.HBM))
        aliases = {len(args): 0}
        args.append(before)

    in_specs += [pl.BlockSpec(memory_space=pltpu.HBM)] * len(after)
    args += after

    def kernel(*refs):
        correlate_kernel(steps, len(own), whole, *refs)

    first = steps[0][0]
    if whole:
        grid = (2,)
        out_spec = pl.BlockSpec((2, 1, ROWS, 1024), lambda g, y: (g, b, 0, 0))
    else:
        grid = (2, len(steps))
        out_spec = pl.BlockSpec((2, 1, ROWS, 256), lambda g, e, y: (g, b, 0, lax.rem(y[0] + first + e, 4)))
    return pl.pallas_call(
        kernel,
        out_shape=jax.ShapeDtypeStruct((4, 4, ROWS, 1024), F32),
        grid_spec=pltpu.PrefetchScalarGridSpec(
            num_scalar_prefetch=1, grid=grid, in_specs=in_specs, out_specs=out_spec
        ),
        input_output_aliases=aliases,
        compiler_params=pltpu.CompilerParams(vmem_limit_bytes=60 * 1024 * 1024),
        cost_estimate=pl.CostEstimate(flops=len(steps) * 160000000, bytes_accessed=6 << 20, transcendentals=0),
        name="correlate",
    )(*args)


def body(v, window):
    groups = lax.axis_size("tm")
    ring = lax.axis_size("inp")
    tables = [jnp.asarray(t) for t in dft_tables()]
    place = lax.axis_index("inp").astype(jnp.int32).reshape(1)
    later = [(i, i + 1) for i in range(groups - 1)]

    def up(x):
        return lax.ppermute(x, "inp", [(i, (i + 1) % ring) for i in range(ring)])

    def down(x):
        return lax.ppermute(x, "inp", [(i, (i - 1) % ring) for i in range(ring)])

    def swap(x):
        return lax.all_to_all(x, "tm", split_axis=0, concat_axis=0, tiled=True)

    halo = []
    for inputs in (range(0, 128), range(128, 256)):
        (passed,) = spectra(v, window, tables, (4, 5, 6), ((1, 3, 2, 0),), False, inputs)
        halo.append(lax.ppermute(passed, "tm", later))
    own = spectra(v, window, tables, (0, 1, 2, 3), ((1,), (3,), (2,), (0,)), True)
    lower, upper, half = (0, 0, 0), (1, 0, 0), (16, 32, LANES)

    (early,) = combine(own[3:], halo, (3,), 1)
    (rows,) = combine(own[:3], halo, (0, 1, 2), 1, (early,))
    late = swap(rows)
    left, right = up(early), down(early)
    first, second = take([(left, half, lower), (right, half, upper)])
    early = pack(early, {1: [right], 2: [up(first), down(second)], 3: [left]})
    odd, even = take([(late, (32, 64, LANES), (0, 0, 0)), (late, (32, 32, LANES), (0, 2, 0))])
    odd_left, odd_right = up(odd), down(odd)
    even_left, even_right = up(even), down(even)
    early = swap(early)

    whole = (32, 32, LANES)
    first, second = take([(odd_left, whole, (0, 0, 0)), (odd_right, whole, (0, 1, 0))])
    odd_far = up(first), down(second)
    out = correlate(place, 0, early, {0: [], 1: [early], 2: [early], 3: [early]}, None, True)
    first, second = take([(even_left, half, lower), (even_right, half, upper)], (out,))
    even_far = [up(first), down(second)]
    out = correlate(place, 2, even, {0: [], 1: [even_right], 3: [even_left]}, out, True)
    for k in range(2):
        planes = {0: [], 1: [odd_right], 2: [odd_far[k]], 3: [odd_left]}
        out = correlate(place, 2 * k + 1, odd, planes, out, True, k)
    out = correlate(place, 2, even, {2: even_far}, out, False)
    return out.reshape(16, ROWS, 1024)


def solution(mesh):
    in_specs = (P("inp", "tm", None), P())
    out_specs = P("tm", "inp", None)
    return jax.shard_map(body, mesh=mesh, in_specs=in_specs, out_specs=out_specs, check_vma=False)
```

```python
import numpy as np

import jax
import jax.numpy as jnp
from jax import lax
from jax.experimental import pallas as pl
from jax.experimental.pallas import tpu as pltpu
from jax.sharding import PartitionSpec as P

FRAME = 2048
TAPS = 4
CH_FIRST = 512
QUARTER = FRAME // 4
CLASSES = 4
F32 = jnp.float32
BF16 = jnp.bfloat16
ROWS = 256
LANES = 256
VMEM = 48 * 1024 * 1024


def halves(x):
    high = x.astype(BF16)
    return high, (x - high.astype(F32)).astype(BF16)


def dft_tables():
    tables = []
    index = np.arange(QUARTER)
    for b in range(CLASSES):
        bins = CH_FIRST + b + CLASSES * np.arange(128)
        phase = (bins[:, None] * index[None, :]) % FRAME
        turn = np.exp(-2j * np.pi / FRAME * phase)
        if b % 2:
            turn = np.concatenate([turn, turn * (-1j if b == 1 else 1j)], axis=1)
        tables.append(np.stack([turn.real, turn.imag], axis=1).reshape(2 * len(bins), -1))
    both = np.concatenate(tables, axis=1)
    high = both.astype(BF16)
    return high, (both - high.astype(np.float64)).astype(BF16)


def spectra_kernel(times, groups, fine, inputs, v_hbm, w_ref, *refs):
    n = 2 if fine else 1
    tables_hbm, refs = refs[:n], refs[n:]
    outs, refs = refs[: len(groups)], refs[len(groups) :]
    frames, high, low, v_ref = refs[:4]
    tables = refs[4 : 4 + n]
    v_sem, table_sem = refs[4 + n :]
    classes = [b for group in groups for b in group]
    block = ROWS // TAPS
    sub = 16
    v_copies = [
        pltpu.make_async_copy(
            v_hbm.at[pl.ds(inputs.start + i * block, block)], v_ref.at[pl.ds(i * block, block)], v_sem.at[i]
        )
        for i in range(len(inputs) // block)
    ]
    table_copies = [pltpu.make_async_copy(tables_hbm[k], tables[k], table_sem.at[k]) for k in range(n)]
    for copy in v_copies + table_copies:
        copy.start()

    to = lax.broadcasted_iota(jnp.int32, (ROWS, ROWS), 0)
    at = lax.broadcasted_iota(jnp.int32, (ROWS, ROWS), 1)
    sort = jnp.where(at == (to % block) * TAPS + to // block, 1.0, 0.0).astype(BF16)

    def per_block(i):
        v_copies[i].wait()
        x = v_ref[pl.ds(i * block, block)].reshape(ROWS, FRAME)
        frames[...] = jnp.dot(sort, x, preferred_element_type=F32)

        def per_rows(r, carry):
            for col in range(QUARTER // 128):
                spans = [pl.ds(m * QUARTER + col * 128, 128) for m in range(4)]
                taps = [[w_ref[pl.ds(j, 1), span] for span in spans] for j in range(TAPS)]
                parts = [
                    [frames[pl.ds(s * block + r * sub, sub), span] for span in spans]
                    for s in range(TAPS)
                ]
                for slot, t in enumerate(times):
                    u = []
                    for m in range(4):
                        terms = [taps[j][m] * parts[t - j][m] for j in range(TAPS) if 0 <= t - j < TAPS]
                        total = terms[0]
                        for term in terms[1:]:
                            total = total + term
                        u.append(total)
                    even, odd = u[0] + u[2], u[1] + u[3]
                    folded = {}
                    if 0 in classes:
                        folded[0] = even + odd
                    if 2 in classes:
                        folded[1] = even - odd
                    if 1 in classes or 3 in classes:
                        folded[2] = u[0] - u[2]
                        folded[3] = u[1] - u[3]
                    for f, value in folded.items():
                        where = slot, pl.ds(i * block + r * sub, sub), pl.ds(f * QUARTER + col * 128, 128)
                        if fine:
                            high[where], low[where] = halves(value)
                        else:
                            high[where] = value.astype(BF16)
            return carry

        lax.fori_loop(0, block // sub, per_rows, 0)

    for i in range(len(inputs) // block):
        per_block(i)
    spans = [slice(0, 512), slice(1024, 2048), slice(512, 1024), slice(1024, 2048)]
    columns = [slice(0, 512), slice(512, 1536), slice(1536, 2048), slice(2048, 3072)]
    contract = (((1,), (1,)), ((), ()))
    for copy in table_copies:
        copy.wait()

    def per_time(slot, carry):
        for b in classes:
            h = high[slot, :, spans[b]]
            table = tables[0][:, columns[b]]
            total = lax.dot_general(table, h, contract, preferred_element_type=F32)
            if fine:
                l = low[slot, :, spans[b]]
                total += lax.dot_general(table, l, contract, preferred_element_type=F32)
                total += lax.dot_general(tables[1][:, columns[b]], h, contract, preferred_element_type=F32)
            for group, out in zip(groups, outs):
                if b in group:
                    out[group.index(b) * len(times) + slot] = total.astype(out.dtype)
        return carry

    lax.fori_loop(0, len(times), per_time, 0)


def spectra(v, window, tables, times, groups, fine, inputs=range(ROWS)):
    def kernel(*refs):
        spectra_kernel(times, groups, fine, inputs, *refs)

    n, size = len(times), len(inputs)
    tables = tables if fine else tables[:1]
    anywhere = pl.BlockSpec(memory_space=pltpu.HBM)
    return pl.pallas_call(
        kernel,
        out_shape=[jax.ShapeDtypeStruct((n * len(g), 256, size), F32 if fine else BF16) for g in groups],
        in_specs=[anywhere, pl.BlockSpec()] + [anywhere] * len(tables),
        scratch_shapes=[
            pltpu.VMEM((ROWS, FRAME), F32),
            pltpu.VMEM((n, size, FRAME), BF16),
            pltpu.VMEM((n if fine else 1, size, FRAME), BF16),
            pltpu.VMEM((size, TAPS, FRAME), BF16),
            *[pltpu.VMEM(t.shape, BF16) for t in tables],
            pltpu.SemaphoreType.DMA((size // (ROWS // TAPS),)),
            pltpu.SemaphoreType.DMA((len(tables),)),
        ],
        compiler_params=pltpu.CompilerParams(vmem_limit_bytes=VMEM),
        cost_estimate=pl.CostEstimate(flops=n * sum(map(len, groups)) * 300000000, bytes_accessed=12 << 20, transcendentals=0),
        name="spectra",
    )(v, window, *tables)


def combine_kernel(order, parts, *refs):
    own, halo = refs[: len(order)], refs[len(order) : len(order) + 2]
    rows = refs[-1]
    outs = refs[len(refs) - 1 - parts : -1]
    size = 32 // parts
    for k, halo_at in enumerate(order):
        for half in range(LANES // 128):
            span = pl.ds(half * 128, 128)
            for t in range(TAPS):
                value = own[k][t, :, span]
                if t < TAPS - 1:
                    value = value + halo[half][halo_at * (TAPS - 1) + t].astype(F32)
                rows[half, pl.ds(t, 256, stride=TAPS), :] = value
            for part in range(parts):
                value = rows[half, pl.ds(part * size * 32, size * 32)].astype(BF16)
                outs[part][:, pl.ds(k * 32, 32), span] = value.reshape(size, 32, 128)


def combine(own, halo, order, parts, after=()):
    n = len(order)

    def kernel(*refs):
        combine_kernel(order, parts, *refs)

    return pl.pallas_call(
        kernel,
        out_shape=[jax.ShapeDtypeStruct((32 // parts, 32 * n, LANES), BF16)] * parts,
        in_specs=[pl.BlockSpec()] * (n + 2) + [pl.BlockSpec(memory_space=pltpu.HBM)] * len(after),
        scratch_shapes=[pltpu.VMEM((LANES // 128, 1024, 128), F32)],
        compiler_params=pltpu.CompilerParams(vmem_limit_bytes=VMEM),
        cost_estimate=pl.CostEstimate(flops=n << 20, bytes_accessed=n * (2 << 20), transcendentals=0),
        name="combine",
    )(*own, *halo, *after)


def take(parts, after=()):
    def kernel(*refs):
        for k in range(len(parts)):
            refs[len(refs) - len(parts) + k][...] = refs[k][...]

    in_specs = [pl.BlockSpec(shape, lambda g, at=at: at) for _, shape, at in parts]
    out_specs = [pl.BlockSpec(shape, lambda g: (0, 0, 0)) for _, shape, _ in parts]
    return pl.pallas_call(
        kernel,
        out_shape=[jax.ShapeDtypeStruct(shape, BF16) for _, shape, _ in parts],
        grid=(1,),
        in_specs=in_specs + [pl.BlockSpec(memory_space=pltpu.HBM)] * len(after),
        out_specs=out_specs,
        compiler_params=pltpu.CompilerParams(vmem_limit_bytes=VMEM),
        cost_estimate=pl.CostEstimate(flops=0, bytes_accessed=2 << 20, transcendentals=0),
        name="take",
    )(*[array for array, _, _ in parts], *after)


def pack_kernel(own, right, far_a, far_b, left, *refs):
    out = refs[-1]
    out[:, 0:32] = own[...]
    out[:, 32:64] = right[...]
    out[:, 96:128] = left[...]

    @pl.when(pl.program_id(0) < 2)
    def _():
        out[:, 64:96] = far_a[...]

    @pl.when(pl.program_id(0) >= 2)
    def _():
        out[:, 64:96] = far_b[...]


def pack(own, planes, after=()):
    part = (8, 32, LANES)
    whole = pl.BlockSpec(part, lambda g: (g, 0, 0))
    return pl.pallas_call(
        pack_kernel,
        out_shape=jax.ShapeDtypeStruct((32, 128, LANES), BF16),
        grid=(4,),
        in_specs=[
            whole,
            whole,
            pl.BlockSpec(part, lambda g: (jnp.minimum(g, 1), 0, 0)),
            pl.BlockSpec(part, lambda g: (jnp.maximum(g - 2, 0), 0, 0)),
            whole,
        ]
        + [pl.BlockSpec(memory_space=pltpu.HBM)] * len(after),
        out_specs=pl.BlockSpec((8, 128, LANES), lambda g: (g, 0, 0)),
        compiler_params=pltpu.CompilerParams(vmem_limit_bytes=VMEM),
        cost_estimate=pl.CostEstimate(flops=0, bytes_accessed=4 << 20, transcendentals=0),
        name="pack",
    )(own, *planes[1], *planes[2], *planes[3], *after)


def correlate_kernel(steps, n_own, whole, place, *refs):
    out = refs[-1]
    y = place[0]
    scale = 1.0 / 128
    ids = lax.broadcasted_iota(jnp.int32, (8, 1), 0)
    sign = jnp.where(ids < 4, 1.0, -1.0)
    row = lax.broadcasted_iota(jnp.int32, (ROWS, ROWS), 0)
    col = lax.broadcasted_iota(jnp.int32, (ROWS, ROWS), 1)

    def pair(ref):
        return ref[...].astype(F32).reshape(ref.shape[0], 2, 8, LANES)

    def flat(x):
        return x.reshape(x.shape[0] * 8, LANES)

    def times_of(plane, other):
        return jnp.dot(plane, other, preferred_element_type=F32) * scale

    mine = [pair(ref) for ref in refs[:n_own]]
    planes = []
    for i in range(2):
        p = jnp.concatenate([x[:, i] for x in mine], axis=0)
        flipped = pltpu.roll(p, 4, 1) * sign
        if whole:
            planes.append((flat(p).astype(BF16).T, flat(flipped).astype(BF16).T))
        else:
            planes.append((p, flipped))

    def products(step, pieces):
        pieces = [pair(refs[k]) for k in pieces]
        q = lax.rem(y + step, 4)
        for i in range(2):
            real, imag = planes[i]
            if step == 0:
                same = jnp.concatenate([flat(x[:, i]) for x in mine], axis=0).astype(BF16)
                yield i, y, jnp.where(row <= col, times_of(real, same), times_of(imag, same))
            else:
                plane = jnp.where(q < y, imag, real)
                if not whole:
                    plane = flat(plane).astype(BF16).T
                other = jnp.concatenate([flat(x[:, i]) for x in pieces], axis=0).astype(BF16)
                yield i, q, times_of(plane, other)

    if whole:
        for step, pieces in steps:
            for i, q, value in products(step, pieces):
                out[i, 0, :, pl.ds(pl.multiple_of(q * 256, 256), 256)] = value
    else:
        for e, (step, pieces) in enumerate(steps):

            @pl.when(pl.program_id(1) == e)
            def _():
                for i, _, value in products(step, pieces):
                    out[i, 0] = value


def correlate(place, b, own, others, before, whole, base=0, after=()):
    def spec(array, step):
        row = {32: 0, 64: base, 128: step}[array.shape[1]]
        return pl.BlockSpec((array.shape[0], 16, LANES), lambda g, *rest: (0, 2 * row + g, 0))

    if not isinstance(own, (list, tuple)):
        own = [own]
    in_specs = [spec(array, 0) for array in own]
    args = [place, *own]
    steps = []
    for step, arrays in others.items():
        steps.append((step, tuple(range(len(args) - 1, len(args) - 1 + len(arrays)))))
        for array in arrays:
            in_specs.append(spec(array, step))
            args.append(array)
    aliases = {}
    if before is not None:
        in_specs.append(pl.BlockSpec(memory_space=pltpu.HBM))
        aliases = {len(args): 0}
        args.append(before)

    in_specs += [pl.BlockSpec(memory_space=pltpu.HBM)] * len(after)
    args += after

    def kernel(*refs):
        correlate_kernel(steps, len(own), whole, *refs)

    first = steps[0][0]
    if whole:
        grid = (2,)
        out_spec = pl.BlockSpec((2, 1, ROWS, 1024), lambda g, y: (g, b, 0, 0))
    else:
        grid = (2, len(steps))
        out_spec = pl.BlockSpec((2, 1, ROWS, 256), lambda g, e, y: (g, b, 0, lax.rem(y[0] + first + e, 4)))
    return pl.pallas_call(
        kernel,
        out_shape=jax.ShapeDtypeStruct((4, 4, ROWS, 1024), F32),
        grid_spec=pltpu.PrefetchScalarGridSpec(
            num_scalar_prefetch=1, grid=grid, in_specs=in_specs, out_specs=out_spec
        ),
        input_output_aliases=aliases,
        compiler_params=pltpu.CompilerParams(vmem_limit_bytes=60 * 1024 * 1024),
        cost_estimate=pl.CostEstimate(flops=len(steps) * 160000000, bytes_accessed=6 << 20, transcendentals=0),
        name="correlate",
    )(*args)


def body(v, window):
    groups = lax.axis_size("tm")
    ring = lax.axis_size("inp")
    tables = [jnp.asarray(t) for t in dft_tables()]
    place = lax.axis_index("inp").astype(jnp.int32).reshape(1)
    later = [(i, i + 1) for i in range(groups - 1)]

    def up(x):
        return lax.ppermute(x, "inp", [(i, (i + 1) % ring) for i in range(ring)])

    def down(x):
        return lax.ppermute(x, "inp", [(i, (i - 1) % ring) for i in range(ring)])

    def swap(x):
        return lax.all_to_all(x, "tm", split_axis=0, concat_axis=0, tiled=True)

    halo = []
    for inputs in (range(0, 128), range(128, 256)):
        (passed,) = spectra(v, window, tables, (4, 5, 6), ((1, 3, 2, 0),), False, inputs)
        halo.append(lax.ppermute(passed, "tm", later))
    own = spectra(v, window, tables, (0, 1, 2, 3), ((1,), (3,), (2,), (0,)), True)
    lower, upper, half = (0, 0, 0), (1, 0, 0), (16, 32, LANES)

    (early,) = combine(own[3:], halo, (3,), 1)
    (rows,) = combine(own[:3], halo, (0, 1, 2), 1, (early,))
    late = swap(rows)
    left, right = up(early), down(early)
    first, second = take([(left, half, lower), (right, half, upper)])
    early = pack(early, {1: [right], 2: [up(first), down(second)], 3: [left]})
    odd, even = take([(late, (32, 64, LANES), (0, 0, 0)), (late, (32, 32, LANES), (0, 2, 0))])
    odd_left, odd_right = up(odd), down(odd)
    even_left, even_right = up(even), down(even)
    early = swap(early)

    whole = (32, 32, LANES)
    first, second = take([(odd_left, whole, (0, 0, 0)), (odd_right, whole, (0, 1, 0))])
    odd_far = up(first), down(second)
    near = {0: [], 1: [odd_right], 3: [odd_left]}
    out = correlate(place, 0, early, {0: [], 1: [early], 2: [early], 3: [early]}, None, True)
    out = correlate(place, 1, odd, near, out, True, 0)
    first, second = take([(even_left, half, lower), (even_right, half, upper)], (out,))
    even_far = [up(first), down(second)]
    out = correlate(place, 3, odd, near, out, True, 1)
    out = correlate(place, 2, even, {0: [], 1: [even_right], 3: [even_left]}, out, True)
    for k in range(2):
        out = correlate(place, 2 * k + 1, odd, {2: [odd_far[k]]}, out, False, k)
    out = correlate(place, 2, even, {2: even_far}, out, False)
    return out.reshape(16, ROWS, 1024)


def solution(mesh):
    in_specs = (P("inp", "tm", None), P())
    out_specs = P("tm", "inp", None)
    return jax.shard_map(body, mesh=mesh, in_specs=in_specs, out_specs=out_specs, check_vma=False)
```

```python
import numpy as np

import jax
import jax.numpy as jnp
from jax import lax
from jax.experimental import pallas as pl
from jax.experimental.pallas import tpu as pltpu
from jax.sharding import PartitionSpec as P

FRAME = 2048
TAPS = 4
CH_FIRST = 512
QUARTER = FRAME // 4
CLASSES = 4
F32 = jnp.float32
BF16 = jnp.bfloat16
ROWS = 256
LANES = 256
VMEM = 48 * 1024 * 1024
LARGE = 60 * 1024 * 1024


def halves(x):
    high = x.astype(BF16)
    return high, (x - high.astype(F32)).astype(BF16)


def dft_tables():
    tables = []
    index = np.arange(QUARTER)
    for b in range(CLASSES):
        bins = CH_FIRST + b + CLASSES * np.arange(128)
        phase = (bins[:, None] * index[None, :]) % FRAME
        turn = np.exp(-2j * np.pi / FRAME * phase)
        if b % 2:
            turn = np.concatenate([turn, turn * (-1j if b == 1 else 1j)], axis=1)
        tables.append(np.stack([turn.real, turn.imag], axis=1).reshape(2 * len(bins), -1))
    both = np.concatenate(tables, axis=1)
    high = both.astype(BF16)
    return high, (both - high.astype(np.float64)).astype(BF16)


def spectra_kernel(times, groups, fine, inputs, v_hbm, w_ref, *refs):
    n = 2 if fine else 1
    tables_hbm, refs = refs[:n], refs[n:]
    outs, refs = refs[: len(groups)], refs[len(groups) :]
    frames, high, low, v_ref = refs[:4]
    tables = refs[4 : 4 + n]
    v_sem, table_sem = refs[4 + n :]
    classes = [b for group in groups for b in group]
    block = ROWS // TAPS
    sub = 16
    v_copies = [
        pltpu.make_async_copy(
            v_hbm.at[pl.ds(inputs.start + i * block, block)], v_ref.at[pl.ds(i * block, block)], v_sem.at[i]
        )
        for i in range(len(inputs) // block)
    ]
    table_copies = [pltpu.make_async_copy(tables_hbm[k], tables[k], table_sem.at[k]) for k in range(n)]
    for copy in v_copies + table_copies:
        copy.start()

    to = lax.broadcasted_iota(jnp.int32, (ROWS, ROWS), 0)
    at = lax.broadcasted_iota(jnp.int32, (ROWS, ROWS), 1)
    sort = jnp.where(at == (to % block) * TAPS + to // block, 1.0, 0.0).astype(BF16)

    def per_block(i):
        v_copies[i].wait()
        x = v_ref[pl.ds(i * block, block)].reshape(ROWS, FRAME)
        frames[...] = jnp.dot(sort, x, preferred_element_type=F32)

        def per_rows(r, carry):
            for col in range(QUARTER // 128):
                spans = [pl.ds(m * QUARTER + col * 128, 128) for m in range(4)]
                taps = [[w_ref[pl.ds(j, 1), span] for span in spans] for j in range(TAPS)]
                parts = [
                    [frames[pl.ds(s * block + r * sub, sub), span] for span in spans]
                    for s in range(TAPS)
                ]
                for slot, t in enumerate(times):
                    u = []
                    for m in range(4):
                        terms = [taps[j][m] * parts[t - j][m] for j in range(TAPS) if 0 <= t - j < TAPS]
                        total = terms[0]
                        for term in terms[1:]:
                            total = total + term
                        u.append(total)
                    even, odd = u[0] + u[2], u[1] + u[3]
                    folded = {}
                    if 0 in classes:
                        folded[0] = even + odd
                    if 2 in classes:
                        folded[1] = even - odd
                    if 1 in classes or 3 in classes:
                        folded[2] = u[0] - u[2]
                        folded[3] = u[1] - u[3]
                    for f, value in folded.items():
                        where = slot, pl.ds(i * block + r * sub, sub), pl.ds(f * QUARTER + col * 128, 128)
                        if fine:
                            high[where], low[where] = halves(value)
                        else:
                            high[where] = value.astype(BF16)
            return carry

        lax.fori_loop(0, block // sub, per_rows, 0)

    for i in range(len(inputs) // block):
        per_block(i)
    spans = [slice(0, 512), slice(1024, 2048), slice(512, 1024), slice(1024, 2048)]
    columns = [slice(0, 512), slice(512, 1536), slice(1536, 2048), slice(2048, 3072)]
    contract = (((1,), (1,)), ((), ()))
    for copy in table_copies:
        copy.wait()

    def per_time(slot, carry):
        for b in classes:
            h = high[slot, :, spans[b]]
            table = tables[0][:, columns[b]]
            total = lax.dot_general(table, h, contract, preferred_element_type=F32)
            if fine:
                l = low[slot, :, spans[b]]
                total += lax.dot_general(table, l, contract, preferred_element_type=F32)
                total += lax.dot_general(tables[1][:, columns[b]], h, contract, preferred_element_type=F32)
            for group, out in zip(groups, outs):
                if b in group:
                    out[group.index(b) * len(times) + slot] = total.astype(out.dtype)
        return carry

    lax.fori_loop(0, len(times), per_time, 0)


def spectra(v, window, tables, times, groups, fine, inputs=range(ROWS)):
    def kernel(*refs):
        spectra_kernel(times, groups, fine, inputs, *refs)

    n, size = len(times), len(inputs)
    tables = tables if fine else tables[:1]
    anywhere = pl.BlockSpec(memory_space=pltpu.HBM)
    return pl.pallas_call(
        kernel,
        out_shape=[jax.ShapeDtypeStruct((n * len(g), 256, size), F32 if fine else BF16) for g in groups],
        in_specs=[anywhere, pl.BlockSpec()] + [anywhere] * len(tables),
        scratch_shapes=[
            pltpu.VMEM((ROWS, FRAME), F32),
            pltpu.VMEM((n, size, FRAME), BF16),
            pltpu.VMEM((n if fine else 1, size, FRAME), BF16),
            pltpu.VMEM((size, TAPS, FRAME), BF16),
            *[pltpu.VMEM(t.shape, BF16) for t in tables],
            pltpu.SemaphoreType.DMA((size // (ROWS // TAPS),)),
            pltpu.SemaphoreType.DMA((len(tables),)),
        ],
        compiler_params=pltpu.CompilerParams(vmem_limit_bytes=VMEM),
        cost_estimate=pl.CostEstimate(flops=n * sum(map(len, groups)) * 300000000, bytes_accessed=12 << 20, transcendentals=0),
        name="spectra",
    )(v, window, *tables)


def combine_kernel(order, parts, *refs):
    own, halo = refs[: len(order)], refs[len(order) : len(order) + 2]
    rows = refs[-1]
    outs = refs[len(refs) - 1 - parts : -1]
    size = 32 // parts
    for k, halo_at in enumerate(order):
        for half in range(LANES // 128):
            span = pl.ds(half * 128, 128)
            for t in range(TAPS):
                value = own[k][t, :, span]
                if t < TAPS - 1:
                    value = value + halo[half][halo_at * (TAPS - 1) + t].astype(F32)
                rows[half, pl.ds(t, 256, stride=TAPS), :] = value
            for part in range(parts):
                value = rows[half, pl.ds(part * size * 32, size * 32)].astype(BF16)
                outs[part][:, pl.ds(k * 32, 32), span] = value.reshape(size, 32, 128)


def combine(own, halo, order, parts, after=()):
    n = len(order)

    def kernel(*refs):
        combine_kernel(order, parts, *refs)

    return pl.pallas_call(
        kernel,
        out_shape=[jax.ShapeDtypeStruct((32 // parts, 32 * n, LANES), BF16)] * parts,
        in_specs=[pl.BlockSpec()] * (n + 2) + [pl.BlockSpec(memory_space=pltpu.HBM)] * len(after),
        scratch_shapes=[pltpu.VMEM((LANES // 128, 1024, 128), F32)],
        compiler_params=pltpu.CompilerParams(vmem_limit_bytes=VMEM),
        cost_estimate=pl.CostEstimate(flops=n << 20, bytes_accessed=n * (2 << 20), transcendentals=0),
        name="combine",
    )(*own, *halo, *after)


def take(parts, after=()):
    def kernel(*refs):
        for k in range(len(parts)):
            refs[len(refs) - len(parts) + k][...] = refs[k][...]

    in_specs = [pl.BlockSpec(shape, lambda g, at=at: at) for _, shape, at in parts]
    out_specs = [pl.BlockSpec(shape, lambda g: (0, 0, 0)) for _, shape, _ in parts]
    return pl.pallas_call(
        kernel,
        out_shape=[jax.ShapeDtypeStruct(shape, BF16) for _, shape, _ in parts],
        grid=(1,),
        in_specs=in_specs + [pl.BlockSpec(memory_space=pltpu.HBM)] * len(after),
        out_specs=out_specs,
        compiler_params=pltpu.CompilerParams(vmem_limit_bytes=VMEM),
        cost_estimate=pl.CostEstimate(flops=0, bytes_accessed=2 << 20, transcendentals=0),
        name="take",
    )(*[array for array, _, _ in parts], *after)


def pack_kernel(own, right, far_a, far_b, left, *refs):
    out = refs[-1]
    out[:, 0:32] = own[...]
    out[:, 32:64] = right[...]
    out[:, 96:128] = left[...]

    @pl.when(pl.program_id(0) < 2)
    def _():
        out[:, 64:96] = far_a[...]

    @pl.when(pl.program_id(0) >= 2)
    def _():
        out[:, 64:96] = far_b[...]


def pack(own, planes, after=()):
    part = (8, 32, LANES)
    whole = pl.BlockSpec(part, lambda g: (g, 0, 0))
    return pl.pallas_call(
        pack_kernel,
        out_shape=jax.ShapeDtypeStruct((32, 128, LANES), BF16),
        grid=(4,),
        in_specs=[
            whole,
            whole,
            pl.BlockSpec(part, lambda g: (jnp.minimum(g, 1), 0, 0)),
            pl.BlockSpec(part, lambda g: (jnp.maximum(g - 2, 0), 0, 0)),
            whole,
        ]
        + [pl.BlockSpec(memory_space=pltpu.HBM)] * len(after),
        out_specs=pl.BlockSpec((8, 128, LANES), lambda g: (g, 0, 0)),
        compiler_params=pltpu.CompilerParams(vmem_limit_bytes=VMEM),
        cost_estimate=pl.CostEstimate(flops=0, bytes_accessed=4 << 20, transcendentals=0),
        name="pack",
    )(own, *planes[1], *planes[2], *planes[3], *after)


def correlate_kernel(steps, n_own, whole, place, *refs):
    out = refs[-1]
    y = place[0]
    scale = 1.0 / 128
    ids = lax.broadcasted_iota(jnp.int32, (8, 1), 0)
    sign = jnp.where(ids < 4, 1.0, -1.0)
    row = lax.broadcasted_iota(jnp.int32, (ROWS, ROWS), 0)
    col = lax.broadcasted_iota(jnp.int32, (ROWS, ROWS), 1)

    def pair(ref):
        return ref[...].astype(F32).reshape(ref.shape[0], 2, 8, LANES)

    def flat(x):
        return x.reshape(x.shape[0] * 8, LANES)

    def times_of(plane, other):
        return jnp.dot(plane, other, preferred_element_type=F32) * scale

    mine = [pair(ref) for ref in refs[:n_own]]
    planes = []
    for i in range(2):
        p = jnp.concatenate([x[:, i] for x in mine], axis=0)
        flipped = pltpu.roll(p, 4, 1) * sign
        if whole:
            planes.append((flat(p).astype(BF16).T, flat(flipped).astype(BF16).T))
        else:
            planes.append((p, flipped))

    def products(step, pieces):
        pieces = [pair(refs[k]) for k in pieces]
        q = lax.rem(y + step, 4)
        for i in range(2):
            real, imag = planes[i]
            if step == 0:
                same = jnp.concatenate([flat(x[:, i]) for x in mine], axis=0).astype(BF16)
                yield i, y, jnp.where(row <= col, times_of(real, same), times_of(imag, same))
            else:
                plane = jnp.where(q < y, imag, real)
                if not whole:
                    plane = flat(plane).astype(BF16).T
                other = jnp.concatenate([flat(x[:, i]) for x in pieces], axis=0).astype(BF16)
                yield i, q, times_of(plane, other)

    if whole:
        for step, pieces in steps:
            for i, q, value in products(step, pieces):
                out[i, 0, :, pl.ds(pl.multiple_of(q * 256, 256), 256)] = value
    else:
        for e, (step, pieces) in enumerate(steps):

            @pl.when(pl.program_id(1) == e)
            def _():
                for i, _, value in products(step, pieces):
                    out[i, 0] = value


def correlate(place, b, own, others, before, whole, base=0, after=(), room=VMEM):
    def spec(array, step):
        row = {32: 0, 64: base, 128: step}[array.shape[1]]
        return pl.BlockSpec((array.shape[0], 16, LANES), lambda g, *rest: (0, 2 * row + g, 0))

    if not isinstance(own, (list, tuple)):
        own = [own]
    in_specs = [spec(array, 0) for array in own]
    args = [place, *own]
    steps = []
    for step, arrays in others.items():
        steps.append((step, tuple(range(len(args) - 1, len(args) - 1 + len(arrays)))))
        for array in arrays:
            in_specs.append(spec(array, step))
            args.append(array)
    aliases = {}
    if before is not None:
        in_specs.append(pl.BlockSpec(memory_space=pltpu.HBM))
        aliases = {len(args): 0}
        args.append(before)

    in_specs += [pl.BlockSpec(memory_space=pltpu.HBM)] * len(after)
    args += after

    def kernel(*refs):
        correlate_kernel(steps, len(own), whole, *refs)

    first = steps[0][0]
    if whole:
        grid = (2,)
        out_spec = pl.BlockSpec((2, 1, ROWS, 1024), lambda g, y: (g, b, 0, 0))
    else:
        grid = (2, len(steps))
        out_spec = pl.BlockSpec((2, 1, ROWS, 256), lambda g, e, y: (g, b, 0, lax.rem(y[0] + first + e, 4)))
    return pl.pallas_call(
        kernel,
        out_shape=jax.ShapeDtypeStruct((4, 4, ROWS, 1024), F32),
        grid_spec=pltpu.PrefetchScalarGridSpec(
            num_scalar_prefetch=1, grid=grid, in_specs=in_specs, out_specs=out_spec
        ),
        input_output_aliases=aliases,
        compiler_params=pltpu.CompilerParams(vmem_limit_bytes=room),
        cost_estimate=pl.CostEstimate(flops=len(steps) * 160000000, bytes_accessed=6 << 20, transcendentals=0),
        name="correlate",
    )(*args)


def far_kernel(place, own, first, second, _, out):
    y = place[0]
    ids = lax.broadcasted_iota(jnp.int32, (8, 1), 0)
    sign = jnp.where(ids < 4, 1.0, -1.0)

    def pair(x):
        return x.astype(F32).reshape(x.shape[0], 2, 8, LANES)

    def flat(x):
        return x.reshape(x.shape[0] * 8, LANES).astype(BF16)

    mine = pair(own[...])
    other = pair(jnp.where(pl.program_id(0) == 0, first[...], second[...]))
    for i in range(2):
        p = mine[:, i]
        plane = jnp.where(lax.rem(y + 2, 4) < y, pltpu.roll(p, 4, 1) * sign, p)
        out[i, 0] = jnp.dot(flat(plane).T, flat(other[:, i]), preferred_element_type=F32) * (1.0 / 128)


def correlate_far(place, own, first, second, before):
    part = (32, 16, LANES)
    in_specs = [
        pl.BlockSpec(part, lambda k, g, y: (0, 2 * k + g, 0)),
        pl.BlockSpec(part, lambda k, g, y: (0, g, 0)),
        pl.BlockSpec(part, lambda k, g, y: (0, g, 0)),
        pl.BlockSpec(memory_space=pltpu.HBM),
    ]
    out_spec = pl.BlockSpec((2, 1, ROWS, 256), lambda k, g, y: (g, 1 + 2 * k, 0, lax.rem(y[0] + 2, 4)))
    return pl.pallas_call(
        far_kernel,
        out_shape=jax.ShapeDtypeStruct((4, 4, ROWS, 1024), F32),
        grid_spec=pltpu.PrefetchScalarGridSpec(
            num_scalar_prefetch=1, grid=(2, 2), in_specs=in_specs, out_specs=out_spec
        ),
        input_output_aliases={4: 0},
        compiler_params=pltpu.CompilerParams(vmem_limit_bytes=VMEM),
        cost_estimate=pl.CostEstimate(flops=320000000, bytes_accessed=6 << 20, transcendentals=0),
        name="correlate_far",
    )(place, own, first, second, before)


def body(v, window):
    groups = lax.axis_size("tm")
    ring = lax.axis_size("inp")
    tables = [jnp.asarray(t) for t in dft_tables()]
    place = lax.axis_index("inp").astype(jnp.int32).reshape(1)
    later = [(i, i + 1) for i in range(groups - 1)]

    def up(x):
        return lax.ppermute(x, "inp", [(i, (i + 1) % ring) for i in range(ring)])

    def down(x):
        return lax.ppermute(x, "inp", [(i, (i - 1) % ring) for i in range(ring)])

    def swap(x):
        return lax.all_to_all(x, "tm", split_axis=0, concat_axis=0, tiled=True)

    halo = []
    for inputs in (range(0, 128), range(128, 256)):
        (passed,) = spectra(v, window, tables, (4, 5, 6), ((1, 3, 2, 0),), False, inputs)
        halo.append(lax.ppermute(passed, "tm", later))
    own = spectra(v, window, tables, (0, 1, 2, 3), ((1,), (3,), (2,), (0,)), True)
    lower, upper, half = (0, 0, 0), (1, 0, 0), (16, 32, LANES)

    (early,) = combine(own[3:], halo, (3,), 1)
    (rows,) = combine(own[:3], halo, (0, 1, 2), 1, (early,))
    late = swap(rows)
    left, right = up(early), down(early)
    first, second = take([(left, half, lower), (right, half, upper)])
    early = pack(early, {1: [right], 2: [up(first), down(second)], 3: [left]})
    odd, even = take([(late, (32, 64, LANES), (0, 0, 0)), (late, (32, 32, LANES), (0, 2, 0))])
    odd_left, odd_right = up(odd), down(odd)
    even_left, even_right = up(even), down(even)
    early = swap(early)

    whole = (32, 32, LANES)
    first, second = take([(odd_left, whole, (0, 0, 0)), (odd_right, whole, (0, 1, 0))])
    odd_far = up(first), down(second)
    near = {0: [], 1: [odd_right], 3: [odd_left]}
    out = correlate(place, 0, early, {0: [], 1: [early], 2: [early], 3: [early]}, None, True, room=LARGE)
    out = correlate(place, 1, odd, near, out, True, 0, room=LARGE)
    first, second = take([(even_left, half, lower), (even_right, half, upper)], (out,))
    even_far = [up(first), down(second)]
    out = correlate(place, 3, odd, near, out, True, 1)
    out = correlate(place, 2, even, {0: [], 1: [even_right], 3: [even_left]}, out, True)
    out = correlate_far(place, odd, *odd_far, out)
    out = correlate(place, 2, even, {2: even_far}, out, False)
    return out.reshape(16, ROWS, 1024)


def solution(mesh):
    in_specs = (P("inp", "tm", None), P())
    out_specs = P("tm", "inp", None)
    return jax.shard_map(body, mesh=mesh, in_specs=in_specs, out_specs=out_specs, check_vma=False)
```

```python
import numpy as np

import jax
import jax.numpy as jnp
from jax import lax
from jax.experimental import pallas as pl
from jax.experimental.pallas import tpu as pltpu
from jax.sharding import PartitionSpec as P

FRAME = 2048
TAPS = 4
CH_FIRST = 512
QUARTER = FRAME // 4
CLASSES = 4
F32 = jnp.float32
BF16 = jnp.bfloat16
ROWS = 256
LANES = 256
VMEM = 48 * 1024 * 1024
LARGE = 62 * 1024 * 1024


def halves(x):
    high = x.astype(BF16)
    return high, (x - high.astype(F32)).astype(BF16)


def dft_tables():
    tables = []
    index = np.arange(QUARTER)
    for b in range(CLASSES):
        bins = CH_FIRST + b + CLASSES * np.arange(128)
        phase = (bins[:, None] * index[None, :]) % FRAME
        turn = np.exp(-2j * np.pi / FRAME * phase)
        if b % 2:
            turn = np.concatenate([turn, turn * (-1j if b == 1 else 1j)], axis=1)
        tables.append(np.stack([turn.real, turn.imag], axis=1).reshape(2 * len(bins), -1))
    both = np.concatenate(tables, axis=1)
    high = both.astype(BF16)
    return high, (both - high.astype(np.float64)).astype(BF16)


def spectra_kernel(times, groups, fine, inputs, v_hbm, w_ref, *refs):
    n = 2 if fine else 1
    tables_hbm, refs = refs[:n], refs[n:]
    outs, refs = refs[: len(groups)], refs[len(groups) :]
    frames, high, low, v_ref = refs[:4]
    tables = refs[4 : 4 + n]
    v_sem, table_sem = refs[4 + n :]
    classes = [b for group in groups for b in group]
    block = ROWS // TAPS
    sub = 16
    v_copies = [
        pltpu.make_async_copy(
            v_hbm.at[pl.ds(inputs.start + i * block, block)], v_ref.at[pl.ds(i * block, block)], v_sem.at[i]
        )
        for i in range(len(inputs) // block)
    ]
    table_copies = [pltpu.make_async_copy(tables_hbm[k], tables[k], table_sem.at[k]) for k in range(n)]
    for copy in v_copies + table_copies:
        copy.start()

    to = lax.broadcasted_iota(jnp.int32, (ROWS, ROWS), 0)
    at = lax.broadcasted_iota(jnp.int32, (ROWS, ROWS), 1)
    sort = jnp.where(at == (to % block) * TAPS + to // block, 1.0, 0.0).astype(BF16)

    def per_block(i):
        v_copies[i].wait()
        x = v_ref[pl.ds(i * block, block)].reshape(ROWS, FRAME)
        frames[...] = jnp.dot(sort, x, preferred_element_type=F32)

        def per_rows(r, carry):
            for col in range(QUARTER // 128):
                spans = [pl.ds(m * QUARTER + col * 128, 128) for m in range(4)]
                taps = [[w_ref[pl.ds(j, 1), span] for span in spans] for j in range(TAPS)]
                parts = [
                    [frames[pl.ds(s * block + r * sub, sub), span] for span in spans]
                    for s in range(TAPS)
                ]
                for slot, t in enumerate(times):
                    u = []
                    for m in range(4):
                        terms = [taps[j][m] * parts[t - j][m] for j in range(TAPS) if 0 <= t - j < TAPS]
                        total = terms[0]
                        for term in terms[1:]:
                            total = total + term
                        u.append(total)
                    even, odd = u[0] + u[2], u[1] + u[3]
                    folded = {}
                    if 0 in classes:
                        folded[0] = even + odd
                    if 2 in classes:
                        folded[1] = even - odd
                    if 1 in classes or 3 in classes:
                        folded[2] = u[0] - u[2]
                        folded[3] = u[1] - u[3]
                    for f, value in folded.items():
                        where = slot, pl.ds(i * block + r * sub, sub), pl.ds(f * QUARTER + col * 128, 128)
                        if fine:
                            high[where], low[where] = halves(value)
                        else:
                            high[where] = value.astype(BF16)
            return carry

        lax.fori_loop(0, block // sub, per_rows, 0)

    for i in range(len(inputs) // block):
        per_block(i)
    spans = [slice(0, 512), slice(1024, 2048), slice(512, 1024), slice(1024, 2048)]
    columns = [slice(0, 512), slice(512, 1536), slice(1536, 2048), slice(2048, 3072)]
    contract = (((1,), (1,)), ((), ()))
    for copy in table_copies:
        copy.wait()

    def per_time(slot, carry):
        for b in classes:
            h = high[slot, :, spans[b]]
            table = tables[0][:, columns[b]]
            total = lax.dot_general(table, h, contract, preferred_element_type=F32)
            if fine:
                l = low[slot, :, spans[b]]
                total += lax.dot_general(table, l, contract, preferred_element_type=F32)
                total += lax.dot_general(tables[1][:, columns[b]], h, contract, preferred_element_type=F32)
            for group, out in zip(groups, outs):
                if b in group:
                    out[group.index(b) * len(times) + slot] = total.astype(out.dtype)
        return carry

    lax.fori_loop(0, len(times), per_time, 0)


def spectra(v, window, tables, times, groups, fine, inputs=range(ROWS)):
    def kernel(*refs):
        spectra_kernel(times, groups, fine, inputs, *refs)

    n, size = len(times), len(inputs)
    tables = tables if fine else tables[:1]
    anywhere = pl.BlockSpec(memory_space=pltpu.HBM)
    return pl.pallas_call(
        kernel,
        out_shape=[jax.ShapeDtypeStruct((n * len(g), 256, size), F32 if fine else BF16) for g in groups],
        in_specs=[anywhere, pl.BlockSpec()] + [anywhere] * len(tables),
        scratch_shapes=[
            pltpu.VMEM((ROWS, FRAME), F32),
            pltpu.VMEM((n, size, FRAME), BF16),
            pltpu.VMEM((n if fine else 1, size, FRAME), BF16),
            pltpu.VMEM((size, TAPS, FRAME), BF16),
            *[pltpu.VMEM(t.shape, BF16) for t in tables],
            pltpu.SemaphoreType.DMA((size // (ROWS // TAPS),)),
            pltpu.SemaphoreType.DMA((len(tables),)),
        ],
        compiler_params=pltpu.CompilerParams(vmem_limit_bytes=VMEM),
        cost_estimate=pl.CostEstimate(flops=n * sum(map(len, groups)) * 300000000, bytes_accessed=12 << 20, transcendentals=0),
        name="spectra",
    )(v, window, *tables)


def combine_kernel(order, parts, *refs):
    own, halo = refs[: len(order)], refs[len(order) : len(order) + 2]
    rows = refs[-1]
    outs = refs[len(refs) - 1 - parts : -1]
    size = 32 // parts
    for k, halo_at in enumerate(order):
        for half in range(LANES // 128):
            span = pl.ds(half * 128, 128)
            for t in range(TAPS):
                value = own[k][t, :, span]
                if t < TAPS - 1:
                    value = value + halo[half][halo_at * (TAPS - 1) + t].astype(F32)
                rows[half, pl.ds(t, 256, stride=TAPS), :] = value
            for part in range(parts):
                value = rows[half, pl.ds(part * size * 32, size * 32)].astype(BF16)
                outs[part][:, pl.ds(k * 32, 32), span] = value.reshape(size, 32, 128)


def combine(own, halo, order, parts, after=()):
    n = len(order)

    def kernel(*refs):
        combine_kernel(order, parts, *refs)

    return pl.pallas_call(
        kernel,
        out_shape=[jax.ShapeDtypeStruct((32 // parts, 32 * n, LANES), BF16)] * parts,
        in_specs=[pl.BlockSpec()] * (n + 2) + [pl.BlockSpec(memory_space=pltpu.HBM)] * len(after),
        scratch_shapes=[pltpu.VMEM((LANES // 128, 1024, 128), F32)],
        compiler_params=pltpu.CompilerParams(vmem_limit_bytes=VMEM),
        cost_estimate=pl.CostEstimate(flops=n << 20, bytes_accessed=n * (2 << 20), transcendentals=0),
        name="combine",
    )(*own, *halo, *after)


def take(parts, after=()):
    def kernel(*refs):
        for k in range(len(parts)):
            refs[len(refs) - len(parts) + k][...] = refs[k][...]

    in_specs = [pl.BlockSpec(shape, lambda g, at=at: at) for _, shape, at in parts]
    out_specs = [pl.BlockSpec(shape, lambda g: (0, 0, 0)) for _, shape, _ in parts]
    return pl.pallas_call(
        kernel,
        out_shape=[jax.ShapeDtypeStruct(shape, BF16) for _, shape, _ in parts],
        grid=(1,),
        in_specs=in_specs + [pl.BlockSpec(memory_space=pltpu.HBM)] * len(after),
        out_specs=out_specs,
        compiler_params=pltpu.CompilerParams(vmem_limit_bytes=VMEM),
        cost_estimate=pl.CostEstimate(flops=0, bytes_accessed=2 << 20, transcendentals=0),
        name="take",
    )(*[array for array, _, _ in parts], *after)


def pack_kernel(own, right, far_a, far_b, left, *refs):
    out = refs[-1]
    out[:, 0:32] = own[...]
    out[:, 32:64] = right[...]
    out[:, 96:128] = left[...]

    @pl.when(pl.program_id(0) < 2)
    def _():
        out[:, 64:96] = far_a[...]

    @pl.when(pl.program_id(0) >= 2)
    def _():
        out[:, 64:96] = far_b[...]


def pack(own, planes, after=()):
    part = (8, 32, LANES)
    whole = pl.BlockSpec(part, lambda g: (g, 0, 0))
    return pl.pallas_call(
        pack_kernel,
        out_shape=jax.ShapeDtypeStruct((32, 128, LANES), BF16),
        grid=(4,),
        in_specs=[
            whole,
            whole,
            pl.BlockSpec(part, lambda g: (jnp.minimum(g, 1), 0, 0)),
            pl.BlockSpec(part, lambda g: (jnp.maximum(g - 2, 0), 0, 0)),
            whole,
        ]
        + [pl.BlockSpec(memory_space=pltpu.HBM)] * len(after),
        out_specs=pl.BlockSpec((8, 128, LANES), lambda g: (g, 0, 0)),
        compiler_params=pltpu.CompilerParams(vmem_limit_bytes=VMEM),
        cost_estimate=pl.CostEstimate(flops=0, bytes_accessed=4 << 20, transcendentals=0),
        name="pack",
    )(own, *planes[1], *planes[2], *planes[3], *after)


def correlate_kernel(steps, n_own, whole, place, *refs):
    out = refs[-1]
    y = place[0]
    scale = 1.0 / 128
    ids = lax.broadcasted_iota(jnp.int32, (8, 1), 0)
    sign = jnp.where(ids < 4, 1.0, -1.0)
    row = lax.broadcasted_iota(jnp.int32, (ROWS, ROWS), 0)
    col = lax.broadcasted_iota(jnp.int32, (ROWS, ROWS), 1)

    def pair(ref):
        return ref[...].astype(F32).reshape(ref.shape[0], 2, 8, LANES)

    def flat(x):
        return x.reshape(x.shape[0] * 8, LANES)

    def times_of(plane, other):
        return jnp.dot(plane, other, preferred_element_type=F32) * scale

    mine = [pair(ref) for ref in refs[:n_own]]
    planes = []
    for i in range(2):
        p = jnp.concatenate([x[:, i] for x in mine], axis=0)
        flipped = pltpu.roll(p, 4, 1) * sign
        if whole:
            planes.append((flat(p).astype(BF16).T, flat(flipped).astype(BF16).T))
        else:
            planes.append((p, flipped))

    def products(step, pieces):
        pieces = [pair(refs[k]) for k in pieces]
        q = lax.rem(y + step, 4)
        for i in range(2):
            real, imag = planes[i]
            if step == 0:
                same = jnp.concatenate([flat(x[:, i]) for x in mine], axis=0).astype(BF16)
                yield i, y, jnp.where(row <= col, times_of(real, same), times_of(imag, same))
            else:
                plane = jnp.where(q < y, imag, real)
                if not whole:
                    plane = flat(plane).astype(BF16).T
                other = jnp.concatenate([flat(x[:, i]) for x in pieces], axis=0).astype(BF16)
                yield i, q, times_of(plane, other)

    if whole:
        for step, pieces in steps:
            for i, q, value in products(step, pieces):
                out[i, 0, :, pl.ds(pl.multiple_of(q * 256, 256), 256)] = value
    else:
        for e, (step, pieces) in enumerate(steps):

            @pl.when(pl.program_id(1) == e)
            def _():
                for i, _, value in products(step, pieces):
                    out[i, 0] = value


def correlate(place, b, own, others, before, whole, base=0, after=(), room=VMEM):
    def spec(array, step):
        row = {32: 0, 64: base, 128: step}[array.shape[1]]
        return pl.BlockSpec((array.shape[0], 16, LANES), lambda g, *rest: (0, 2 * row + g, 0))

    if not isinstance(own, (list, tuple)):
        own = [own]
    in_specs = [spec(array, 0) for array in own]
    args = [place, *own]
    steps = []
    for step, arrays in others.items():
        steps.append((step, tuple(range(len(args) - 1, len(args) - 1 + len(arrays)))))
        for array in arrays:
            in_specs.append(spec(array, step))
            args.append(array)
    aliases = {}
    if before is not None:
        in_specs.append(pl.BlockSpec(memory_space=pltpu.HBM))
        aliases = {len(args): 0}
        args.append(before)

    in_specs += [pl.BlockSpec(memory_space=pltpu.HBM)] * len(after)
    args += after

    def kernel(*refs):
        correlate_kernel(steps, len(own), whole, *refs)

    first = steps[0][0]
    if whole:
        grid = (2,)
        out_spec = pl.BlockSpec((2, 1, ROWS, 1024), lambda g, y: (g, b, 0, 0))
    else:
        grid = (2, len(steps))
        out_spec = pl.BlockSpec((2, 1, ROWS, 256), lambda g, e, y: (g, b, 0, lax.rem(y[0] + first + e, 4)))
    return pl.pallas_call(
        kernel,
        out_shape=jax.ShapeDtypeStruct((4, 4, ROWS, 1024), F32),
        grid_spec=pltpu.PrefetchScalarGridSpec(
            num_scalar_prefetch=1, grid=grid, in_specs=in_specs, out_specs=out_spec
        ),
        input_output_aliases=aliases,
        compiler_params=pltpu.CompilerParams(vmem_limit_bytes=room),
        cost_estimate=pl.CostEstimate(flops=len(steps) * 160000000, bytes_accessed=6 << 20, transcendentals=0),
        name="correlate",
    )(*args)


def far_kernel(place, own, first, second, _, out):
    y = place[0]
    ids = lax.broadcasted_iota(jnp.int32, (8, 1), 0)
    sign = jnp.where(ids < 4, 1.0, -1.0)

    def pair(x):
        return x.astype(F32).reshape(x.shape[0], 2, 8, LANES)

    def flat(x):
        return x.reshape(x.shape[0] * 8, LANES).astype(BF16)

    mine = pair(own[...])
    other = pair(jnp.where(pl.program_id(0) == 0, first[...], second[...]))
    for i in range(2):
        p = mine[:, i]
        plane = jnp.where(lax.rem(y + 2, 4) < y, pltpu.roll(p, 4, 1) * sign, p)
        out[i, 0] = jnp.dot(flat(plane).T, flat(other[:, i]), preferred_element_type=F32) * (1.0 / 128)


def correlate_far(place, own, first, second, before):
    part = (32, 16, LANES)
    in_specs = [
        pl.BlockSpec(part, lambda k, g, y: (0, 2 * k + g, 0)),
        pl.BlockSpec(part, lambda k, g, y: (0, g, 0)),
        pl.BlockSpec(part, lambda k, g, y: (0, g, 0)),
        pl.BlockSpec(memory_space=pltpu.HBM),
    ]
    out_spec = pl.BlockSpec((2, 1, ROWS, 256), lambda k, g, y: (g, 1 + 2 * k, 0, lax.rem(y[0] + 2, 4)))
    return pl.pallas_call(
        far_kernel,
        out_shape=jax.ShapeDtypeStruct((4, 4, ROWS, 1024), F32),
        grid_spec=pltpu.PrefetchScalarGridSpec(
            num_scalar_prefetch=1, grid=(2, 2), in_specs=in_specs, out_specs=out_spec
        ),
        input_output_aliases={4: 0},
        compiler_params=pltpu.CompilerParams(vmem_limit_bytes=VMEM),
        cost_estimate=pl.CostEstimate(flops=320000000, bytes_accessed=6 << 20, transcendentals=0),
        name="correlate_far",
    )(place, own, first, second, before)


def body(v, window):
    groups = lax.axis_size("tm")
    ring = lax.axis_size("inp")
    tables = [jnp.asarray(t) for t in dft_tables()]
    place = lax.axis_index("inp").astype(jnp.int32).reshape(1)
    later = [(i, i + 1) for i in range(groups - 1)]

    def up(x):
        return lax.ppermute(x, "inp", [(i, (i + 1) % ring) for i in range(ring)])

    def down(x):
        return lax.ppermute(x, "inp", [(i, (i - 1) % ring) for i in range(ring)])

    def swap(x):
        return lax.all_to_all(x, "tm", split_axis=0, concat_axis=0, tiled=True)

    halo = []
    for inputs in (range(0, 128), range(128, 256)):
        (passed,) = spectra(v, window, tables, (4, 5, 6), ((1, 3, 2, 0),), False, inputs)
        halo.append(lax.ppermute(passed, "tm", later))
    own = spectra(v, window, tables, (0, 1, 2, 3), ((1,), (3,), (2,), (0,)), True)
    lower, upper, half = (0, 0, 0), (1, 0, 0), (16, 32, LANES)

    (early,) = combine(own[3:], halo, (3,), 1)
    (rows,) = combine(own[:3], halo, (0, 1, 2), 1, (early,))
    late = swap(rows)
    left, right = up(early), down(early)
    first, second = take([(left, half, lower), (right, half, upper)])
    early = pack(early, {1: [right], 2: [up(first), down(second)], 3: [left]})
    odd, even = take([(late, (32, 64, LANES), (0, 0, 0)), (late, (32, 32, LANES), (0, 2, 0))])
    odd_left, odd_right = up(odd), down(odd)
    even_left, even_right = up(even), down(even)
    early = swap(early)

    whole = (32, 32, LANES)
    first, second = take([(odd_left, whole, (0, 0, 0)), (odd_right, whole, (0, 1, 0))])
    odd_far = up(first), down(second)
    near = {0: [], 1: [odd_right], 3: [odd_left]}
    out = correlate(place, 0, early, {0: [], 1: [early], 2: [early], 3: [early]}, None, True, room=LARGE)
    out = correlate(place, 1, odd, near, out, True, 0, room=LARGE)
    first, second = take([(even_left, half, lower), (even_right, half, upper)], (out,))
    even_far = [up(first), down(second)]
    out = correlate(place, 3, odd, near, out, True, 1)
    out = correlate(place, 2, even, {0: [], 1: [even_right], 3: [even_left]}, out, True)
    out = correlate_far(place, odd, *odd_far, out)
    out = correlate(place, 2, even, {2: even_far}, out, False)
    return out.reshape(16, ROWS, 1024)


def solution(mesh):
    in_specs = (P("inp", "tm", None), P())
    out_specs = P("tm", "inp", None)
    return jax.shard_map(body, mesh=mesh, in_specs=in_specs, out_specs=out_specs, check_vma=False)
```
